1024 devices in a mesh: dp: 64 (over z, core), mp: 16 (over x, y).
Axes of the slice: x: 4, y: 4, z: 32, core: 2. Of those that a mesh axis runs over, the one named last changes fastest.
Arguments:
- queries: bfloat16 [32768, 4096], P('dp', 'mp'), may hold values from -6 to 6
- keys: bfloat16 [32768, 512], P('dp'), may hold values from -6 to 6
- values: bfloat16 [32768, 512], P('dp'), may hold values from -6 to 6
- attn_out: bfloat16 [32768, 4096], P('dp', 'mp'), may hold values from -4 to 4
- out_grad: bfloat16 [32768, 4096], P('dp', 'mp'), may hold values from -4 to 4
- lse: bfloat16 [32768, 32], P('dp', 'mp'), may hold values from 0 to 3
- layer_grad: bfloat16 [32768, 4096], P('dp'), may hold values from -0.3125 to 0.3125
- feedback: bfloat16 [64, 4096, 4096], P('dp', None, 'mp'), may hold values from -0.29882812 to 0.29882812
- doc_lengths: int32 [64, 8], P('dp'), may hold values from 1 to 256, 512 in all within a row
- src_order: int32 [64, 64], P('dp'), may hold values from 0 to 63, each once within a row
- dst_order: int32 [64, 64], P('dp'), may hold values from 0 to 63, each once within a row
Outputs:
- query_grad: bfloat16 [32768, 4096], P('dp', 'mp')
- kv_grad: bfloat16 [32768, 1024], P(('dp', 'mp'))
- weight_grad: float32 [4096, 4096], P('dp', 'mp')
The draws below stay inside these ranges and needn't reach their ends.
Inputs may be any that keep to these rules, and one draw needn't show every extreme that they name: Each row of src_order is a permutation: replica r sends exactly one block to each replica d, its block src_order[r, d]. Each row of dst_order is a permutation: every replica receives exactly one block from each replica. `doc_lengths`: each row sums to 512.
All inputs are finite; a program needn't handle non-finite values.
Results may differ from the reference program's by a relative error of at most 0.0095.
Values may be sent and summed in bfloat16 or wider, within the bound.
A program may use at most 64 MiB of HBM per device.

```python
import math
import jax
import jax.numpy as jnp
import numpy as np
from jax import lax

HD = 128
HPD = 2
GROUP = 8
DW = 4096
CR = 8
NDOC = 8
TOK = 512
HQ = 32
KVH = 4
TOKENS = 32768
MAXLEN = 256
N_DP = 64
N_MP = 16


def strengthened(drawn, rng, source, target, parts, factor):
    owner, partner = [(jnp.arange(drawn.shape[dim]) // (drawn.shape[dim] // parts)).reshape([-1 if axis == dim else 1 for axis in range(drawn.ndim)]) for dim in (source, target)]
    chosen = jax.random.permutation(rng, parts)[partner]
    strong = (owner == chosen) | (owner == (partner + parts // 2) % parts)
    return jnp.where(strong, factor * drawn, drawn)


def steps_of(key, shape, cuts, low, largest):
    loudness, own = 1.0, jax.random.fold_in(key, 6)
    for axis_at, shards_of in cuts:
        draws = jnp.exp(jax.random.uniform(jax.random.fold_in(own, axis_at), (shards_of,), jnp.float32, low / len(cuts), largest / len(cuts)))
        loudness = loudness * jnp.repeat(draws, shape[axis_at] // shards_of).reshape([-1 if axis == axis_at else 1 for axis in range(len(shape))])
    return loudness


def length_profile(count, total, limit, skew):
    loads = [(1 << 20) // math.isqrt(rank ** skew) + 1 for rank in range(2, count + 1)]
    rest, counts = total - limit - (count - 1), [1] * (count - 1)
    while rest > 0:
        movable = [i for i in range(count - 1) if counts[i] < limit]
        pool, left = sum([loads[i] for i in movable]), rest
        for i in movable:
            addition = min(limit - counts[i], max(1, left * loads[i] // pool), rest)
            counts[i] = counts[i] + addition
            rest = rest - addition
    return np.array([limit] + counts)


def uneven_parts(rng, number_of, total, most, slope):
    if number_of == 2:
        one = jax.random.randint(rng, (), max(1, total - most), min(most, total - 1) + 1)
        return jnp.stack([one, total - one])
    sizes = jnp.asarray(length_profile(number_of, total, most, slope), jnp.int32)
    pairs = (number_of - 1) // 2
    giver, receiver = sizes[1:1 + 2 * pairs:2], sizes[2:2 + 2 * pairs:2]
    room = jnp.minimum(giver - 1, most - receiver)
    moved = jax.random.randint(jax.random.fold_in(rng, 1), (pairs,), 0, 1 << 20) % (room + 1)
    sizes = sizes.at[1:1 + 2 * pairs:2].set(giver - moved).at[2:2 + 2 * pairs:2].set(receiver + moved)
    return sizes[jax.random.permutation(jax.random.fold_in(rng, 2), number_of)]


def normal_values(key, shape, width, most, pieces=(), kind=jnp.bfloat16):
    level = steps_of(key, shape, pieces, -0.22, 0.18) if pieces else 1.0
    values = jax.random.normal(key, shape, jnp.float32) * width * level
    return jnp.minimum(jnp.maximum(values, -most), most).astype(kind)


def heavy_noise(key, shape, spread, bound, cuts, heavy, kind=jnp.bfloat16):
    result = spread * jax.random.normal(key, shape, jnp.float32)
    if cuts:
        result = result * steps_of(key, shape, cuts, -0.22, 0.18)
    return jnp.clip(strengthened(result, jax.random.fold_in(key, 3), *heavy), -bound, bound).astype(kind)


def setup_inputs(seed: int = 0) -> dict:
    key_list = jax.random.split(jax.random.key(seed), 12)
    queries = normal_values(key_list[0], (TOKENS, HQ * HD), 1.0, 6.0, ((0, 64), (1, 16)))
    keys = normal_values(key_list[1], (TOKENS, KVH * HD), 1.0, 6.0, ((0, 64),))
    values = normal_values(key_list[2], (TOKENS, KVH * HD), 1.0, 6.0, ((0, 64),))
    attn_out = normal_values(key_list[3], (TOKENS, HQ * HD), 0.3, 4.0, ((0, 64), (1, 16)))
    out_grad = normal_values(key_list[4], (TOKENS, HQ * HD), 0.3, 4.0, ((0, 64), (1, 16)))
    lse = jnp.clip(3.0 * jax.random.uniform(key_list[5], (TOKENS, HQ), jnp.float32) ** steps_of(key_list[5], (TOKENS, HQ), ((0, 64), (1, 16)), -0.2, 0.2), 0.0, 3.0).astype(jnp.bfloat16)
    layer_grad = heavy_noise(key_list[6], (TOKENS, DW), 0.02, 0.3125, ((0, 64),), (0, 1, 64, 4.0))
    feedback = normal_values(key_list[7], (N_DP, DW, HQ * HD), 0.05, 0.29882812, ((0, 64), (2, 16)))
    doc_lengths = jax.vmap(lambda own: uneven_parts(own, NDOC, TOK, MAXLEN, 2))(jax.random.split(key_list[8], N_DP)).reshape((N_DP, NDOC)).astype(jnp.int32)
    src_order = jax.vmap(lambda own: jax.random.permutation(own, N_DP))(jax.random.split(key_list[9], N_DP)).reshape((N_DP, N_DP)).astype(jnp.int32)
    dst_order = jax.vmap(lambda own: jax.random.permutation(own, N_DP))(jax.random.split(key_list[10], N_DP)).reshape((N_DP, N_DP)).astype(jnp.int32)
    return dict(queries=queries, keys=keys, values=values, attn_out=attn_out, out_grad=out_grad, lse=lse, layer_grad=layer_grad, feedback=feedback, doc_lengths=doc_lengths, src_order=src_order, dst_order=dst_order)


def quantize_rows(term):
    spans = term.reshape(DW // CR, CR, N_MP, HPD * HD)
    top = jnp.max(jnp.abs(spans), axis=(1, 3), keepdims=True) + 1e-6
    scales = lax.optimization_barrier(top.astype(jnp.bfloat16)).astype(jnp.float32)
    levels = lax.optimization_barrier((spans / scales).astype(jnp.bfloat16)).astype(jnp.float32)
    return (levels * scales).reshape(DW, N_MP * HPD * HD)


def attend_replica(inputs):
    q_rows, k_rows, v_rows, o_rows, do_rows, lse_rows, lengths = inputs
    factor = HD ** -0.5
    q_heads = q_rows.astype(jnp.float32).reshape(TOK, HQ, HD)
    o_heads = o_rows.astype(jnp.float32).reshape(TOK, HQ, HD)
    do_heads = do_rows.astype(jnp.float32).reshape(TOK, HQ, HD)
    k_heads = jnp.repeat(k_rows.astype(jnp.float32).reshape(TOK, KVH, HD), GROUP, axis=1)
    v_heads = jnp.repeat(v_rows.astype(jnp.float32).reshape(TOK, KVH, HD), GROUP, axis=1)
    ends = jnp.cumsum(lengths.astype(jnp.int32))
    positions = jnp.arange(TOK, dtype=jnp.int32)
    segment = jnp.sum((positions[:, None] >= ends[None, :]).astype(jnp.int32), axis=1)
    allowed = (segment[:, None] == segment[None, :]) & (positions[None, :] <= positions[:, None])
    scores = jnp.einsum('qhd,khd->hqk', q_heads, k_heads) * factor
    probs = jnp.where(allowed[None], jnp.exp(scores - lse_rows.astype(jnp.float32).T[:, :, None]), 0.0)
    probs_low = lax.optimization_barrier(probs.astype(jnp.bfloat16)).astype(jnp.float32)
    value_sum = jnp.einsum('hqk,qhd->khd', probs_low, do_heads).reshape(TOK, KVH, GROUP, HD).sum(axis=2)
    dprobs = jnp.einsum('qhd,khd->hqk', do_heads, v_heads)
    delta = jnp.sum(do_heads * o_heads, axis=-1)
    dscores = probs * (dprobs - delta.T[:, :, None])
    dscores_low = lax.optimization_barrier((dscores * factor).astype(jnp.bfloat16)).astype(jnp.float32)
    query_grad = jnp.einsum('hqk,khd->qhd', dscores_low, k_heads).astype(jnp.bfloat16).reshape(TOK, HQ * HD)
    key_sum = jnp.einsum('hqk,qhd->khd', dscores_low, q_heads).reshape(TOK, KVH, GROUP, HD).sum(axis=2)
    kv_grad = jnp.concatenate([key_sum.reshape(TOK, KVH * HD), value_sum.reshape(TOK, KVH * HD)], axis=1)
    return query_grad, kv_grad.astype(jnp.bfloat16)


def reference(queries, keys, values, attn_out, out_grad, lse, layer_grad, feedback, doc_lengths, src_order, dst_order):
    block_rows = TOK // N_DP
    source = dst_order.astype(jnp.int32)
    target = jnp.broadcast_to(jnp.arange(N_DP, dtype=jnp.int32)[:, None], (N_DP, N_DP))
    local = src_order.astype(jnp.int32)[source, target]

    def move(array):
        columns = array.shape[1]
        grouped = array.reshape(N_DP, N_DP, block_rows, columns)
        return grouped[source, local].reshape(N_DP, TOK, columns)

    moved = (move(queries), move(keys), move(values), move(attn_out), move(out_grad), move(lse), doc_lengths)
    query_parts, kv_parts = lax.map(attend_replica, moved)
    query_grad = query_parts.reshape(TOKENS, HQ * HD)
    kv_grad = kv_parts.reshape(TOKENS, 2 * KVH * HD)

    def add_replica(total, inputs):
        grad_rows, out_rows, carried = inputs
        term = jnp.dot(grad_rows.T, out_rows, preferred_element_type=jnp.float32) + carried.astype(jnp.float32)
        return total + quantize_rows(term), None

    weight_grad, _ = lax.scan(add_replica, jnp.zeros((DW, HQ * HD), jnp.float32),
                              (layer_grad.reshape(N_DP, TOK, DW), attn_out.reshape(N_DP, TOK, HQ * HD), feedback))
    return query_grad, kv_grad, weight_grad
```

```python
import functools

import jax
import jax.numpy as jnp
from jax import lax
from jax.experimental import pallas as pl
from jax.experimental.pallas import tpu as pltpu
from jax.sharding import PartitionSpec as P

HD = 128
HPD = 2
GROUP = 8
CR = 8
BR = 8
SHARE = GROUP // HPD
STRIDE = 29
FIRST = 16
MESH = pl.DeviceIdType.MESH


def whole_wait(ref, sem):
    pltpu.make_async_copy(ref, ref, sem).wait()


def kernel(
    n,
    nm,
    src_ref,
    dst_ref,
    len_ref,
    q_ref,
    do_ref,
    o3_ref,
    o_ref,
    lse_ref,
    k_hbm,
    v_hbm,
    lg_hbm,
    fb_hbm,
    qg_ref,
    kvg_ref,
    wg_ref,
    kv_in,
    lg_v,
    fb_v,
    st_cols,
    st_rows,
    qd_send,
    qd_recv,
    kv_send,
    kv_recv,
    st_send,
    st_recv,
    own,
    p_send,
    p_recv,
    r_send,
    r_recv,
    l_send,
    l_recv,
    m_q,
    m_do,
    m_kv,
    dkv,
    g_send,
    g_recv,
    loc_sem,
    qd_s,
    qd_r,
    kv_s,
    kv_r,
    st_s,
    st_r,
    yf_s,
    yf_r,
    p_s,
    p_r,
    r_s,
    r_r,
    l_s,
    l_r,
    g_s,
    g_r,
):
    f32, bf16 = jnp.float32, jnp.bfloat16
    me = lax.axis_index("dp")
    mp = lax.axis_index("mp")
    group, y = mp // SHARE, mp % SHARE
    z, core = me // 2, me % 2
    nz = n // 2
    rows = n * BR
    right_hops, left_hops = nz // 2, nz // 2 - 1
    per_class = n // SHARE

    column = pl.ds(pl.multiple_of(group * HD, HD), HD)
    k_copy = pltpu.make_async_copy(k_hbm.at[:, :, column], kv_in.at[0], loc_sem.at[0])
    v_copy = pltpu.make_async_copy(v_hbm.at[:, :, column], kv_in.at[1], loc_sem.at[1])
    lg_copy = pltpu.make_async_copy(lg_hbm, lg_v, loc_sem.at[2])
    fb_copy = pltpu.make_async_copy(fb_hbm, fb_v, loc_sem.at[3])
    k_copy.start()
    v_copy.start()
    lg_copy.start()
    fb_copy.start()

    barrier = pltpu.get_barrier_semaphore()

    def greet_dp(k, _):
        pl.semaphore_signal(barrier, 1, device_id=((me + k) % n, mp), device_id_type=MESH)
        return 0

    def greet_mp(k, _):
        pl.semaphore_signal(barrier, 1, device_id=(me, (mp + k) % nm), device_id_type=MESH)
        return 0

    lax.fori_loop(1, n, greet_dp, 0)
    lax.fori_loop(1, nm, greet_mp, 0)

    product = (do_ref[...].astype(f32) * o3_ref[...].astype(f32)).reshape(rows, HPD * HD)
    delta0 = jnp.sum(product[:, :HD], axis=1, keepdims=True)
    delta1 = jnp.sum(product[:, HD:], axis=1, keepdims=True)
    lse = lse_ref[...]
    lane = lax.broadcasted_iota(jnp.int32, (rows, HD), 1)
    st_cols[...] = jnp.where(
        lane == 0,
        lse[:, 0:1],
        jnp.where(
            lane == 1,
            lse[:, 1:2],
            jnp.where(lane == 2, delta0, jnp.where(lane == 3, delta1, 0.0)),
        ),
    )
    packed = st_cols[pl.ds(0, n, stride=BR), :]
    for r in range(1, BR):
        packed = packed + pltpu.roll(st_cols[pl.ds(r, n, stride=BR), :], 4 * r, 1)
    st_rows[...] = packed

    k_copy.wait()
    v_copy.wait()

    def pack(d, _):
        block = src_ref[0, d]
        kv_send[d] = jnp.concatenate([kv_in[0, block], kv_in[1, block]], axis=0)
        st_send[d] = st_rows[pl.ds(block, 1), :]
        qb = q_ref[block]
        db = do_ref[block]
        qd_send[d] = jnp.concatenate([qb[:, :HD], qb[:, HD:], db[:, :HD], db[:, HD:]], axis=0)
        return 0

    lax.fori_loop(0, n, pack, 0)

    pl.semaphore_wait(barrier, n - 1 + nm - 1)

    def kv_slot(source, dest):
        return ((source + dest) % SHARE) * per_class + source // SHARE

    own_slot = kv_slot(me, me)
    has_self = (me + me) % SHARE == y

    def send_kv(j, _):
        d = SHARE * ((me // SHARE + j) % per_class) + (y + SHARE - me % SHARE) % SHARE
        slot = y * per_class + me // SHARE

        @pl.when(d == me)
        def _():
            pltpu.make_async_copy(kv_send.at[me], kv_recv.at[slot], kv_r).start()

        @pl.when(d != me)
        def _():
            pltpu.make_async_remote_copy(
                kv_send.at[d], kv_recv.at[slot], kv_s, kv_r, device_id=(d, mp), device_id_type=MESH
            ).start()

        return 0

    lax.fori_loop(0, per_class, send_kv, 0)

    pltpu.make_async_copy(qd_send.at[me], qd_recv.at[me], qd_r).start()
    pltpu.make_async_copy(st_send.at[me], st_recv.at[me], st_r).start()

    def send_block(t, _):
        d = (me + t * STRIDE) % n
        pltpu.make_async_remote_copy(
            qd_send.at[d], qd_recv.at[me], qd_s, qd_r, device_id=(d, mp), device_id_type=MESH
        ).start()
        pltpu.make_async_remote_copy(
            st_send.at[d], st_recv.at[me], st_s, st_r, device_id=(d, mp), device_id_type=MESH
        ).start()
        return 0

    first = min(FIRST, n)
    lax.fori_loop(1, first, send_block, 0)
    per_step = -(-(n - first) // right_hops)

    lg_copy.wait()
    fb_copy.wait()
    partner = me + 1 - 2 * core

    def partner_copy(g):
        return pltpu.make_async_remote_copy(
            p_send.at[pl.ds(2 * g, 2)],
            p_recv.at[pl.ds(2 * g, 2)],
            p_s.at[g],
            p_r.at[g],
            device_id=(partner, mp),
            device_id_type=MESH,
        )

    def make_term(g, _):
        start = pl.multiple_of(g * 256, 256)
        term = lax.dot_general(
            lg_v[:, pl.ds(start, 256)],
            o_ref[...],
            (((0,), (0,)), ((), ())),
            preferred_element_type=f32,
        )
        term = term + fb_v[pl.ds(start, 256), :].astype(f32)
        spans = term.reshape(256 // CR, CR, HPD * HD)
        top = jnp.max(jnp.max(jnp.abs(spans), axis=1, keepdims=True), axis=2, keepdims=True)
        scale = (top + 1e-06).astype(bf16).astype(f32)
        level = (spans / scale).astype(bf16).astype(f32)
        value = (level * scale).reshape(4, 64, HPD * HD)
        for chip in range(2):
            even, odd = value[2 * chip], value[2 * chip + 1]
            own[2 * g + chip] = jnp.where(core == 0, even, odd)
            p_send[2 * g + chip] = jnp.where(core == 0, odd, even).astype(bf16)
        partner_copy(g).start()
        return 0

    lax.fori_loop(0, nz // 2, make_term, 0)

    def partner_wait(g, _):
        partner_copy(g).wait()
        return 0

    lax.fori_loop(0, nz // 2, partner_wait, 0)

    def right_copy(s):
        return pltpu.make_async_remote_copy(
            r_send.at[s],
            r_recv.at[s],
            r_s.at[s],
            r_r.at[s],
            device_id=(((z + 1) % nz) * 2 + core, mp),
            device_id_type=MESH,
        )

    def left_copy(s):
        return pltpu.make_async_remote_copy(
            l_send.at[s],
            l_recv.at[s],
            l_s.at[s],
            l_r.at[s],
            device_id=(((z + nz - 1) % nz) * 2 + core, mp),
            device_id_type=MESH,
        )

    def own_sum(chip):
        return own[chip] + p_recv[chip].astype(f32)

    def more_blocks(s):
        begin = jnp.minimum(first + s * per_step, n)
        end = jnp.minimum(begin + per_step, n)
        lax.fori_loop(begin, end, send_block, 0)

    r_send[0] = own_sum((z + right_hops) % nz).astype(bf16)
    right_copy(0).start()
    if left_hops > 0:
        l_send[0] = own_sum((z + nz - left_hops) % nz).astype(bf16)
        left_copy(0).start()
    more_blocks(0)

    def step(s, _):
        right_copy(s - 1).wait_recv()
        total = own_sum((z + right_hops - s) % nz) + r_recv[s - 1].astype(f32)
        r_send[s] = total.astype(bf16)
        right_copy(s).start()

        @pl.when(s < left_hops)
        def _():
            left_copy(s - 1).wait_recv()
            other = own_sum((z + nz - left_hops + s) % nz) + l_recv[s - 1].astype(f32)
            l_send[s] = other.astype(bf16)
            left_copy(s).start()

        more_blocks(s)
        return 0

    half = max(right_hops // 2, 1)
    lax.fori_loop(1, half, step, 0)

    whole_wait(kv_recv.at[pl.ds(0, per_class)], kv_r)
    share = pl.ds(y * per_class, per_class)
    forwards = [
        pltpu.make_async_remote_copy(
            kv_recv.at[share],
            kv_recv.at[share],
            yf_s.at[t - 1],
            yf_r.at[t - 1],
            device_id=(me, group * SHARE + (y + t) % SHARE),
            device_id_type=MESH,
        )
        for t in range(1, SHARE)
    ]
    for forward in forwards:
        forward.start()

    lax.fori_loop(half, right_hops, step, 0)

    right_copy(right_hops - 1).wait_recv()
    total = own_sum(z) + r_recv[right_hops - 1].astype(f32)
    if left_hops > 0:
        left_copy(left_hops - 1).wait_recv()
        total = total + l_recv[left_hops - 1].astype(f32)
    wg_ref[...] = total

    for forward in forwards:
        forward.wait()

    def unpack_kv(i, _):
        parts = []
        for b in range(2):
            source = dst_ref[0, 2 * i + b]
            parts.append(kv_recv[kv_slot(source, me)])
        at = pl.ds(pl.multiple_of(2 * BR * i, 2 * BR), 2 * BR)
        for j in range(2):
            m_kv[j, at, :] = jnp.concatenate([part[BR * j : BR * (j + 1)] for part in parts], axis=0)
        return 0

    lax.fori_loop(0, n // 2, unpack_kv, 0)

    whole_wait(st_recv, st_r)
    whole_wait(qd_recv, qd_r)

    def unpack(i, _):
        parts = []
        for b in range(2):
            source = dst_ref[0, 2 * i + b]
            st_rows[pl.ds(2 * i + b, 1), :] = st_recv[source]
            parts.append(qd_recv[source])
        at = pl.ds(pl.multiple_of(2 * BR * i, 2 * BR), 2 * BR)
        for h in range(HPD):
            m_q[h, at, :] = jnp.concatenate([part[BR * h : BR * (h + 1)] for part in parts], axis=0)
            low = BR * (HPD + h)
            m_do[h, at, :] = jnp.concatenate([part[low : low + BR] for part in parts], axis=0)
        return 0

    lax.fori_loop(0, n // 2, unpack, 0)

    arrived = st_rows[...]
    st_cols[pl.ds(0, n, stride=BR), :] = arrived
    for r in range(1, BR):
        st_cols[pl.ds(r, n, stride=BR), :] = pltpu.roll(arrived, HD - 4 * r, 1)
    stats = st_cols[...].T[0:8]

    def segments(positions):
        end = len_ref[0, 0]
        found = (positions >= end).astype(jnp.int32)
        for j in range(1, len_ref.shape[1]):
            end = end + len_ref[0, j]
            found = found + (positions >= end).astype(jnp.int32)
        return found

    factor = HD ** (-0.5)
    nt = (((1,), (1,)), ((), ()))
    tn = (((0,), (0,)), ((), ()))
    dkv[...] = jnp.zeros_like(dkv)
    half_rows = rows // 2
    for part in range(2):
        low, high = part * half_rows, (part + 1) * half_rows
        k_pos = lax.broadcasted_iota(jnp.int32, (high, 1), 0)
        q_pos = lax.broadcasted_iota(jnp.int32, (1, half_rows), 1) + low
        allowed = (segments(k_pos) == segments(q_pos)) & (k_pos <= q_pos)
        k_head = m_kv[0, 0:high, :]
        v_head = m_kv[1, 0:high, :]
        for h in range(HPD):
            q_head = m_q[h, low:high, :]
            do_head = m_do[h, low:high, :]
            scores = lax.dot_general(k_head, q_head, nt, preferred_element_type=f32) * factor
            probs = jnp.where(allowed, jnp.exp(scores - stats[h : h + 1, low:high]), 0.0)
            dkv[0:high, HD:] += jnp.dot(probs.astype(bf16), do_head, preferred_element_type=f32)
            dprobs = lax.dot_general(v_head, do_head, nt, preferred_element_type=f32)
            delta = stats[HPD + h : HPD + h + 1, low:high]
            dscores = (probs * (dprobs - delta) * factor).astype(bf16)
            dkv[0:high, :HD] += jnp.dot(dscores, q_head, preferred_element_type=f32)
            q_grad = lax.dot_general(dscores, k_head, tn, preferred_element_type=f32)
            qg_ref[low:high, HD * h : HD * (h + 1)] = q_grad.astype(bf16)

    kept = rows // nm
    g_send[...] = dkv[...].astype(bf16).reshape(nm, kept, 2 * HD)
    pltpu.make_async_copy(g_send.at[mp], g_recv.at[mp], g_r).start()

    def send_grad(k, _):
        other = (mp + k) % nm
        pltpu.make_async_remote_copy(
            g_send.at[other], g_recv.at[mp], g_s, g_r, device_id=(me, other), device_id_type=MESH
        ).start()
        return 0

    lax.fori_loop(1, nm, send_grad, 0)

    whole_wait(qd_send.at[pl.ds(0, n - 1)], qd_s)
    whole_wait(st_send.at[pl.ds(0, n - 1)], st_s)

    @pl.when(has_self)
    def _():
        whole_wait(kv_send.at[pl.ds(0, per_class - 1)], kv_s)

    @pl.when(jnp.logical_not(has_self))
    def _():
        whole_wait(kv_send.at[pl.ds(0, per_class)], kv_s)

    def ring_sent(s, _):
        right_copy(s).wait_send()

        @pl.when(s < left_hops)
        def _():
            left_copy(s).wait_send()

        return 0

    lax.fori_loop(0, right_hops, ring_sent, 0)

    whole_wait(g_recv, g_r)
    groups = nm // SHARE
    for x in range(groups):
        total = g_recv[SHARE * x].astype(f32)
        for j in range(1, SHARE):
            total = total + g_recv[SHARE * x + j].astype(f32)
        total = total.astype(bf16)
        kvg_ref[:, HD * x : HD * (x + 1)] = total[:, :HD]
        kvg_ref[:, HD * (groups + x) : HD * (groups + x + 1)] = total[:, HD:]
    whole_wait(g_send.at[pl.ds(0, nm - 1)], g_s)


def body(
    queries,
    keys,
    values,
    attn_out,
    out_grad,
    lse,
    layer_grad,
    feedback,
    doc_lengths,
    src_order,
    dst_order,
):
    n, nm = lax.axis_size("dp"), lax.axis_size("mp")
    rows, cols = queries.shape
    nz = n // 2
    right_hops, left_hops = nz // 2, max(nz // 2 - 1, 1)
    kept = rows // nm
    owned = layer_grad.shape[1] // n
    f32, bf16 = jnp.float32, jnp.bfloat16
    smem = pl.BlockSpec(memory_space=pltpu.SMEM)
    vmem = pl.BlockSpec(memory_space=pltpu.VMEM)
    hbm = pl.BlockSpec(memory_space=pl.ANY)
    dma = pltpu.SemaphoreType.DMA

    def blocks(array):
        return array.reshape(n, BR, array.shape[1])

    return pl.pallas_call(
        functools.partial(kernel, n, nm),
        out_shape=(
            jax.ShapeDtypeStruct((rows, cols), bf16),
            jax.ShapeDtypeStruct((kept, 2 * keys.shape[1]), bf16),
            jax.ShapeDtypeStruct((owned, cols), f32),
        ),
        in_specs=[smem] * 3 + [vmem] * 5 + [hbm] * 4,
        out_specs=(vmem, vmem, vmem),
        scratch_shapes=[
            pltpu.VMEM((2, n, BR, HD), bf16),
            pltpu.VMEM(layer_grad.shape, bf16),
            pltpu.VMEM(feedback.shape[1:], bf16),
            pltpu.VMEM((rows, HD), f32),
            pltpu.VMEM((n, HD), f32),
            pltpu.VMEM((n, 4 * BR, HD), bf16),
            pltpu.VMEM((n, 4 * BR, HD), bf16),
            pltpu.VMEM((n, 2 * BR, HD), bf16),
            pltpu.VMEM((n, 2 * BR, HD), bf16),
            pltpu.VMEM((n, 1, HD), f32),
            pltpu.VMEM((n, 1, HD), f32),
            pltpu.VMEM((nz, owned, cols), f32),
            pltpu.VMEM((nz, owned, cols), bf16),
            pltpu.VMEM((nz, owned, cols), bf16),
            pltpu.VMEM((right_hops, owned, cols), bf16),
            pltpu.VMEM((right_hops, owned, cols), bf16),
            pltpu.VMEM((left_hops, owned, cols), bf16),
            pltpu.VMEM((left_hops, owned, cols), bf16),
            pltpu.VMEM((HPD, rows, HD), bf16),
            pltpu.VMEM((HPD, rows, HD), bf16),
            pltpu.VMEM((2, rows, HD), bf16),
            pltpu.VMEM((rows, 2 * HD), f32),
            pltpu.VMEM((nm, kept, 2 * HD), bf16),
            pltpu.VMEM((nm, kept, 2 * HD), bf16),
            dma((4,)),
            dma,
            dma,
            dma,
            dma,
            dma,
            dma,
            dma((SHARE - 1,)),
            dma((SHARE - 1,)),
            dma((nz // 2,)),
            dma((nz // 2,)),
            dma((right_hops,)),
            dma((right_hops,)),
            dma((left_hops,)),
            dma((left_hops,)),
            dma,
            dma,
        ],
        compiler_params=pltpu.CompilerParams(
            collective_id=0, has_side_effects=True, vmem_limit_bytes=48 * 1024 * 1024
        ),
    )(
        src_order,
        dst_order,
        doc_lengths,
        blocks(queries),
        blocks(out_grad),
        blocks(attn_out),
        attn_out,
        lse.astype(f32),
        blocks(keys),
        blocks(values),
        layer_grad,
        feedback[0],
    )


def solution(mesh):
    return jax.shard_map(
        body,
        mesh=mesh,
        in_specs=(
            P("dp", "mp"),
            P("dp", None),
            P("dp", None),
            P("dp", "mp"),
            P("dp", "mp"),
            P("dp", "mp"),
            P("dp", None),
            P("dp", None, "mp"),
            P("dp", None),
            P("dp", None),
            P("dp", None),
        ),
        out_specs=(P("dp", "mp"), P(("dp", "mp"), None), P("dp", "mp")),
        check_vma=False,
    )
```

```python
import functools

import jax
import jax.numpy as jnp
from jax import lax
from jax.experimental import pallas as pl
from jax.experimental.pallas import tpu as pltpu
from jax.sharding import PartitionSpec as P

HD = 128
HPD = 2
GROUP = 8
CR = 8
BR = 8
SHARE = GROUP // HPD
STRIDE = 29
SPAN = 2
FIRST = 8
PER = 8
BEFORE = 7
PASS = 4
MESH = pl.DeviceIdType.MESH


def whole_wait(ref, sem):
    pltpu.make_async_copy(ref, ref, sem).wait()


def kernel(
    n,
    nm,
    src_hbm,
    dst_hbm,
    len_hbm,
    q_hbm,
    do_hbm,
    o_hbm,
    lse_hbm,
    k_hbm,
    v_hbm,
    lg_hbm,
    fb_hbm,
    qg_ref,
    kvg_ref,
    wg_ref,
    qg_out,
    kvg_out,
    wg_out,
    src_ref,
    dst_ref,
    len_ref,
    q_ref,
    do_ref,
    o_ref,
    lse_ref,
    kv_in,
    lg_v,
    fb_v,
    st_cols,
    st_rows,
    qd_send,
    qd_recv,
    kv_send,
    kv_recv,
    st_send,
    st_recv,
    own,
    p_send,
    p_recv,
    rc_send,
    rc_recv,
    rj_send,
    rj_recv,
    lc_send,
    lc_recv,
    lj_send,
    lj_recv,
    m_q,
    m_do,
    m_kv,
    dkv,
    g_send,
    g_recv,
    loc_sem,
    qd_s,
    qd_r,
    kv_s,
    kv_r,
    st_s,
    st_r,
    yf_s,
    yf_r,
    p_s,
    p_r,
    rc_s,
    rc_r,
    rj_s,
    rj_r,
    lc_s,
    lc_r,
    lj_s,
    lj_r,
    g_s,
    g_r,
):
    f32, bf16 = jnp.float32, jnp.bfloat16
    me = lax.axis_index("dp")
    mp = lax.axis_index("mp")
    group, y = mp // SHARE, mp % SHARE
    z, core = me // 2, me % 2
    nz = n // 2
    rows = n * BR
    per_class = n // SHARE

    column = pl.ds(pl.multiple_of(group * HD, HD), HD)
    loads = [
        (do_hbm, do_ref),
        (o_hbm, o_ref),
        (lse_hbm, lse_ref),
        (src_hbm, src_ref),
        (q_hbm, q_ref),
        (k_hbm.at[:, :, column], kv_in.at[0]),
        (v_hbm.at[:, :, column], kv_in.at[1]),
        (dst_hbm, dst_ref),
        (len_hbm, len_ref),
        (lg_hbm, lg_v),
        (fb_hbm, fb_v),
    ]
    loads = [pltpu.make_async_copy(a, b, loc_sem.at[i]) for i, (a, b) in enumerate(loads)]
    for load in loads:
        load.start()

    barrier = pltpu.get_barrier_semaphore()

    def greet_dp(k, _):
        pl.semaphore_signal(barrier, 1, device_id=((me + k) % n, mp), device_id_type=MESH)
        return 0

    def greet_mp(k, _):
        pl.semaphore_signal(barrier, 1, device_id=(me, (mp + k) % nm), device_id_type=MESH)
        return 0

    lax.fori_loop(1, n, greet_dp, 0)
    lax.fori_loop(1, nm, greet_mp, 0)

    for load in loads[:3]:
        load.wait()
    product = do_ref[...].astype(f32).reshape(rows, HPD * HD) * o_ref[...].astype(f32)
    delta0 = jnp.sum(product[:, :HD], axis=1, keepdims=True)
    delta1 = jnp.sum(product[:, HD:], axis=1, keepdims=True)
    lse = jnp.concatenate(
        [lse_ref[...].astype(f32), jnp.zeros((HD - HPD, rows), f32)], axis=0
    ).T
    lane = lax.broadcasted_iota(jnp.int32, (rows, HD), 1)
    st_cols[...] = jnp.where(lane == 2, delta0, jnp.where(lane == 3, delta1, lse))
    packed = st_cols[pl.ds(0, n, stride=BR), :]
    for r in range(1, BR):
        packed = packed + pltpu.roll(st_cols[pl.ds(r, n, stride=BR), :], 4 * r, 1)
    st_rows[...] = packed

    for load in loads[3:7]:
        load.wait()

    pl.semaphore_wait(barrier, n - 1 + nm - 1)

    def kv_slot(source, dest):
        return ((source + dest) % SHARE) * per_class + source // SHARE

    has_self = (me + me) % SHARE == y

    def send_kv(j, _):
        d = SHARE * ((me // SHARE + j) % per_class) + (y + SHARE - me % SHARE) % SHARE
        slot = y * per_class + me // SHARE
        block = src_ref[0, d]
        kv_send[d] = jnp.concatenate([kv_in[0, block], kv_in[1, block]], axis=0)

        @pl.when(d == me)
        def _():
            pltpu.make_async_copy(kv_send.at[me], kv_recv.at[slot], kv_r).start()

        @pl.when(d != me)
        def _():
            pltpu.make_async_remote_copy(
                kv_send.at[d], kv_recv.at[slot], kv_s, kv_r, device_id=(d, mp), device_id_type=MESH
            ).start()

        return 0

    lax.fori_loop(0, per_class, send_kv, 0)

    def pack(d):
        block = src_ref[0, d]
        st_send[d] = st_rows[pl.ds(block, 1), :]
        qb = q_ref[block]
        db = do_ref[block]
        qd_send[d] = jnp.concatenate([qb[:, :HD], qb[:, HD:], db[:, :HD], db[:, HD:]], axis=0)

    pack(me)
    pltpu.make_async_copy(qd_send.at[me], qd_recv.at[me], qd_r).start()
    pltpu.make_async_copy(st_send.at[me], st_recv.at[me], st_r).start()

    def send_block(t, _):
        d = (me + t * STRIDE) % n
        pack(d)
        pltpu.make_async_remote_copy(
            qd_send.at[d], qd_recv.at[me], qd_s, qd_r, device_id=(d, mp), device_id_type=MESH
        ).start()
        pltpu.make_async_remote_copy(
            st_send.at[d], st_recv.at[me], st_s, st_r, device_id=(d, mp), device_id_type=MESH
        ).start()
        return 0

    first = min(FIRST, n)
    lax.fori_loop(1, first, send_block, 0)

    for load in loads[7:]:
        load.wait()
    partner = me + 1 - 2 * core

    def partner_copy(g):
        return pltpu.make_async_remote_copy(
            p_send.at[pl.ds(2 * g, 2)],
            p_recv.at[pl.ds(2 * g, 2)],
            p_s.at[g],
            p_r.at[g],
            device_id=(partner, mp),
            device_id_type=MESH,
        )

    def make_term(g, _):
        start = pl.multiple_of(g * 256, 256)
        term = lax.dot_general(
            lg_v[:, pl.ds(start, 256)],
            o_ref[...],
            (((0,), (0,)), ((), ())),
            preferred_element_type=f32,
        )
        term = term + fb_v[pl.ds(start, 256), :].astype(f32)
        spans = term.reshape(256 // CR, CR, HPD * HD)
        top = jnp.max(jnp.max(jnp.abs(spans), axis=1, keepdims=True), axis=2, keepdims=True)
        scale = (top + 1e-06).astype(bf16).astype(f32)
        level = (spans / scale).astype(bf16).astype(f32)
        value = (level * scale).reshape(4, 64, HPD * HD)
        for chip in range(2):
            even, odd = value[2 * chip], value[2 * chip + 1]
            own[2 * g + chip] = jnp.where(core == 0, even, odd)
            p_send[2 * g + chip] = jnp.where(core == 0, odd, even).astype(bf16)
        partner_copy(g).start()
        return 0

    lax.fori_loop(0, nz // 2, make_term, 0)

    def partner_wait(g, _):
        partner_copy(g).wait()
        return 0

    lax.fori_loop(0, nz // 2, partner_wait, 0)

    sides = (
        (1, nz // 2, rc_send, rc_recv, rj_send, rj_recv, rc_s, rc_r, rj_s, rj_r),
        (-1, nz // 2 - 1, lc_send, lc_recv, lj_send, lj_recv, lc_s, lc_r, lj_s, lj_r),
    )

    def chip_at(distance):
        return (z + distance % nz) % nz

    def device_at(distance):
        return (chip_at(distance) * 2 + core, mp)

    def own_sum(distance):
        chip = chip_at(distance)
        return own[chip] + p_recv[chip].astype(f32)

    def walk_count(limit, j):
        return len([k for k in range(nz) if SPAN * k + j <= limit])

    def walk_copy(side, t):
        sign, limit, send, recv, _, _, s_sem, r_sem, _, _ = side
        part = pl.ds(0, walk_count(limit, SPAN - t))
        return pltpu.make_async_remote_copy(
            send.at[t, part],
            recv.at[t, part],
            s_sem.at[t],
            r_sem.at[t],
            device_id=device_at(sign),
            device_id_type=MESH,
        )

    def jump_copy(side, u):
        sign, limit, _, _, send, recv, _, _, s_sem, r_sem = side
        last = u == walk_count(limit, 1) - 1
        return pltpu.make_async_remote_copy(
            send.at[u],
            recv.at[u],
            s_sem.at[u],
            r_sem.at[u],
            device_id=device_at(sign if last else sign * SPAN),
            device_id_type=MESH,
        )

    def walk(side, t):
        sign, limit, send, recv = side[:4]
        j = SPAN - t
        came = walk_count(limit, j + 1) if t > 0 else 0
        if came:
            walk_copy(side, t - 1).wait_recv()
        for k in range(walk_count(limit, j)):
            total = own_sum(sign * (SPAN * k + j))
            if k < came:
                total = total + recv[t - 1, k].astype(f32)
            send[t, k] = total.astype(bf16)
        if walk_count(limit, j):
            walk_copy(side, t).start()

    def jump(side, u):
        sign, limit, _, walked, send, recv = side[:6]
        k = walk_count(limit, 1) - 1 - u
        if k < 0:
            return
        came = walk_count(limit, 2)
        if u == 0 and came:
            walk_copy(side, SPAN - 2).wait_recv()
        total = own_sum(sign * (SPAN * k + 1))
        if k < came:
            total = total + walked[SPAN - 2, k].astype(f32)
        if u > 0:
            jump_copy(side, u - 1).wait_recv()
            total = total + recv[u - 1].astype(f32)
        send[u] = total.astype(bf16)
        jump_copy(side, u).start()

    jumps = walk_count(nz // 2, 1)
    stage_count = SPAN - 1 + jumps
    before = min(BEFORE, stage_count)

    def stage(i):
        for side in sides:
            if i < SPAN - 1:
                walk(side, i)
            else:
                jump(side, i - (SPAN - 1))

    for i in range(min(PASS, before)):
        stage(i)
        lax.fori_loop(min(first + i * PER, n), min(first + (i + 1) * PER, n), send_block, 0)

    whole_wait(kv_recv.at[pl.ds(0, per_class)], kv_r)
    share = pl.ds(y * per_class, per_class)
    forwards = [
        pltpu.make_async_remote_copy(
            kv_recv.at[share],
            kv_recv.at[share],
            yf_s.at[t - 1],
            yf_r.at[t - 1],
            device_id=(me, group * SHARE + (y + t) % SHARE),
            device_id_type=MESH,
        )
        for t in range(1, SHARE)
    ]
    for forward in forwards:
        forward.start()

    for i in range(min(PASS, before), before):
        stage(i)
        lax.fori_loop(min(first + i * PER, n), min(first + (i + 1) * PER, n), send_block, 0)
    lax.fori_loop(min(first + before * PER, n), n, send_block, 0)

    for forward in forwards:
        forward.wait()

    def unpack_kv(i, _):
        parts = []
        for b in range(2):
            source = dst_ref[0, 2 * i + b]
            parts.append(kv_recv[kv_slot(source, me)])
        at = pl.ds(pl.multiple_of(2 * BR * i, 2 * BR), 2 * BR)
        for j in range(2):
            m_kv[j, at, :] = jnp.concatenate([part[BR * j : BR * (j + 1)] for part in parts], axis=0)
        return 0

    lax.fori_loop(0, n // 2, unpack_kv, 0)

    whole_wait(st_recv, st_r)
    whole_wait(qd_recv, qd_r)

    def unpack(i, _):
        parts = []
        for b in range(2):
            source = dst_ref[0, 2 * i + b]
            st_rows[pl.ds(2 * i + b, 1), :] = st_recv[source]
            parts.append(qd_recv[source])
        at = pl.ds(pl.multiple_of(2 * BR * i, 2 * BR), 2 * BR)
        for h in range(HPD):
            m_q[h, at, :] = jnp.concatenate([part[BR * h : BR * (h + 1)] for part in parts], axis=0)
            low = BR * (HPD + h)
            m_do[h, at, :] = jnp.concatenate([part[low : low + BR] for part in parts], axis=0)
        return 0

    lax.fori_loop(0, n // 2, unpack, 0)

    arrived = st_rows[...]
    st_cols[pl.ds(0, n, stride=BR), :] = arrived
    for r in range(1, BR):
        st_cols[pl.ds(r, n, stride=BR), :] = pltpu.roll(arrived, HD - 4 * r, 1)
    stats = st_cols[...].T[0:8]

    def segments(positions):
        end = len_ref[0, 0]
        found = (positions >= end).astype(jnp.int32)
        for j in range(1, len_ref.shape[1]):
            end = end + len_ref[0, j]
            found = found + (positions >= end).astype(jnp.int32)
        return found

    factor = HD ** (-0.5)
    nt = (((1,), (1,)), ((), ()))
    tn = (((0,), (0,)), ((), ()))
    dkv[...] = jnp.zeros_like(dkv)
    half_rows = rows // 2
    for part in range(2):
        low, high = part * half_rows, (part + 1) * half_rows
        k_pos = lax.broadcasted_iota(jnp.int32, (high, 1), 0)
        q_pos = lax.broadcasted_iota(jnp.int32, (1, half_rows), 1) + low
        allowed = (segments(k_pos) == segments(q_pos)) & (k_pos <= q_pos)
        k_head = m_kv[0, 0:high, :]
        v_head = m_kv[1, 0:high, :]
        for h in range(HPD):
            q_head = m_q[h, low:high, :]
            do_head = m_do[h, low:high, :]
            scores = lax.dot_general(k_head, q_head, nt, preferred_element_type=f32) * factor
            probs = jnp.where(allowed, jnp.exp(scores - stats[h : h + 1, low:high]), 0.0)
            dkv[0:high, HD:] += jnp.dot(probs.astype(bf16), do_head, preferred_element_type=f32)
            dprobs = lax.dot_general(v_head, do_head, nt, preferred_element_type=f32)
            delta = stats[HPD + h : HPD + h + 1, low:high]
            dscores = (probs * (dprobs - delta) * factor).astype(bf16)
            dkv[0:high, :HD] += jnp.dot(dscores, q_head, preferred_element_type=f32)
            q_grad = lax.dot_general(dscores, k_head, tn, preferred_element_type=f32)
            qg_out[low:high, HD * h : HD * (h + 1)] = q_grad.astype(bf16)

    qg_store = pltpu.make_async_copy(qg_out, qg_ref, loc_sem.at[0])
    qg_store.start()

    kept = rows // nm
    g_send[...] = dkv[...].astype(bf16).reshape(nm, kept, 2 * HD)
    pltpu.make_async_copy(g_send.at[mp], g_recv.at[mp], g_r).start()

    def send_grad(k, _):
        other = (mp + k) % nm
        pltpu.make_async_remote_copy(
            g_send.at[other], g_recv.at[mp], g_s, g_r, device_id=(me, other), device_id_type=MESH
        ).start()
        return 0

    lax.fori_loop(1, nm, send_grad, 0)

    for i in range(before, stage_count):
        stage(i)
    total = own_sum(0)
    for side in sides:
        count = walk_count(side[1], 1)
        if count:
            jump_copy(side, count - 1).wait_recv()
            total = total + side[5][count - 1].astype(f32)
    wg_out[...] = total
    wg_store = pltpu.make_async_copy(wg_out, wg_ref, loc_sem.at[1])
    wg_store.start()

    whole_wait(qd_send.at[pl.ds(0, n - 1)], qd_s)
    whole_wait(st_send.at[pl.ds(0, n - 1)], st_s)

    @pl.when(has_self)
    def _():
        whole_wait(kv_send.at[pl.ds(0, per_class - 1)], kv_s)

    @pl.when(jnp.logical_not(has_self))
    def _():
        whole_wait(kv_send.at[pl.ds(0, per_class)], kv_s)

    for side in sides:
        for t in range(SPAN - 1):
            if walk_count(side[1], SPAN - t):
                walk_copy(side, t).wait_send()
        for u in range(walk_count(side[1], 1)):
            jump_copy(side, u).wait_send()

    whole_wait(g_recv, g_r)
    groups = nm // SHARE
    for x in range(groups):
        total = g_recv[SHARE * x].astype(f32)
        for j in range(1, SHARE):
            total = total + g_recv[SHARE * x + j].astype(f32)
        total = total.astype(bf16)
        kvg_out[:, HD * x : HD * (x + 1)] = total[:, :HD]
        kvg_out[:, HD * (groups + x) : HD * (groups + x + 1)] = total[:, HD:]
    kvg_store = pltpu.make_async_copy(kvg_out, kvg_ref, loc_sem.at[2])
    kvg_store.start()
    whole_wait(g_send.at[pl.ds(0, nm - 1)], g_s)
    qg_store.wait()
    wg_store.wait()
    kvg_store.wait()


def body(
    queries,
    keys,
    values,
    attn_out,
    out_grad,
    lse,
    layer_grad,
    feedback,
    doc_lengths,
    src_order,
    dst_order,
):
    n, nm = lax.axis_size("dp"), lax.axis_size("mp")
    rows, cols = queries.shape
    nz = n // 2
    jumps = -(-(nz // 2) // SPAN)
    kept = rows // nm
    owned = layer_grad.shape[1] // n
    f32, bf16 = jnp.float32, jnp.bfloat16
    hbm = pl.BlockSpec(memory_space=pltpu.HBM)
    dma = pltpu.SemaphoreType.DMA
    walks = [pltpu.VMEM((SPAN - 1, jumps, owned, cols), bf16)] * 2
    walks += [pltpu.VMEM((jumps, owned, cols), bf16)] * 2
    walk_sems = [dma((SPAN - 1,))] * 2 + [dma((jumps,))] * 2

    def blocks(array):
        return array.reshape(n, BR, array.shape[1])

    outs = (
        jax.ShapeDtypeStruct((rows, cols), bf16),
        jax.ShapeDtypeStruct((kept, 2 * keys.shape[1]), bf16),
        jax.ShapeDtypeStruct((owned, cols), f32),
    )
    return pl.pallas_call(
        functools.partial(kernel, n, nm),
        out_shape=outs,
        in_specs=[hbm] * 11,
        out_specs=(hbm, hbm, hbm),
        scratch_shapes=[
            *(pltpu.VMEM(out.shape, out.dtype) for out in outs),
            pltpu.SMEM(src_order.shape, jnp.int32),
            pltpu.SMEM(dst_order.shape, jnp.int32),
            pltpu.SMEM(doc_lengths.shape, jnp.int32),
            pltpu.VMEM((n, BR, cols), bf16),
            pltpu.VMEM((n, BR, cols), bf16),
            pltpu.VMEM((rows, cols), bf16),
            pltpu.VMEM((HPD, rows), bf16),
            pltpu.VMEM((2, n, BR, HD), bf16),
            pltpu.VMEM(layer_grad.shape, bf16),
            pltpu.VMEM(feedback.shape[1:], bf16),
            pltpu.VMEM((rows, HD), f32),
            pltpu.VMEM((n, HD), f32),
            pltpu.VMEM((n, 4 * BR, HD), bf16),
            pltpu.VMEM((n, 4 * BR, HD), bf16),
            pltpu.VMEM((n, 2 * BR, HD), bf16),
            pltpu.VMEM((n, 2 * BR, HD), bf16),
            pltpu.VMEM((n, 1, HD), f32),
            pltpu.VMEM((n, 1, HD), f32),
            pltpu.VMEM((nz, owned, cols), f32),
            pltpu.VMEM((nz, owned, cols), bf16),
            pltpu.VMEM((nz, owned, cols), bf16),
            *walks,
            *walks,
            pltpu.VMEM((HPD, rows, HD), bf16),
            pltpu.VMEM((HPD, rows, HD), bf16),
            pltpu.VMEM((2, rows, HD), bf16),
            pltpu.VMEM((rows, 2 * HD), f32),
            pltpu.VMEM((nm, kept, 2 * HD), bf16),
            pltpu.VMEM((nm, kept, 2 * HD), bf16),
            dma((11,)),
            dma,
            dma,
            dma,
            dma,
            dma,
            dma,
            dma((SHARE - 1,)),
            dma((SHARE - 1,)),
            dma((nz // 2,)),
            dma((nz // 2,)),
            *walk_sems,
            *walk_sems,
            dma,
            dma,
        ],
        compiler_params=pltpu.CompilerParams(
            collective_id=0, has_side_effects=True, vmem_limit_bytes=60 * 1024 * 1024
        ),
    )(
        src_order,
        dst_order,
        doc_lengths,
        blocks(queries),
        blocks(out_grad),
        attn_out,
        lse.T,
        blocks(keys),
        blocks(values),
        layer_grad,
        feedback[0],
    )


def solution(mesh):
    return jax.shard_map(
        body,
        mesh=mesh,
        in_specs=(
            P("dp", "mp"),
            P("dp", None),
            P("dp", None),
            P("dp", "mp"),
            P("dp", "mp"),
            P("dp", "mp"),
            P("dp", None),
            P("dp", None, "mp"),
            P("dp", None),
            P("dp", None),
            P("dp", None),
        ),
        out_specs=(P("dp", "mp"), P(("dp", "mp"), None), P("dp", "mp")),
        check_vma=False,
    )
```

```python
import functools

import jax
import jax.numpy as jnp
from jax import lax
from jax.experimental import pallas as pl
from jax.experimental.pallas import tpu as pltpu
from jax.sharding import PartitionSpec as P

HD = 128
HPD = 2
GROUP = 8
CR = 8
BR = 8
SHARE = GROUP // HPD
STRIDE = 29
SPAN = 2
FIRST = 8
PER = 8
BEFORE = 8
PASS = 4
MESH = pl.DeviceIdType.MESH


def whole_wait(ref, sem):
    pltpu.make_async_copy(ref, ref, sem).wait()


def kernel(
    n,
    nm,
    order_hbm,
    q_hbm,
    do_hbm,
    o_hbm,
    lse_hbm,
    k_hbm,
    v_hbm,
    lg_hbm,
    fb_hbm,
    qg_ref,
    kvg_ref,
    wg_ref,
    qg_out,
    kvg_out,
    wg_out,
    order_ref,
    q_ref,
    do_ref,
    o_ref,
    lse_ref,
    kv_in,
    lg_v,
    fb_v,
    st_cols,
    st_rows,
    qd_send,
    qd_recv,
    kv_send,
    kv_recv,
    st_send,
    st_recv,
    own,
    p_send,
    p_recv,
    rc_send,
    rc_recv,
    rj_send,
    rj_recv,
    lc_send,
    lc_recv,
    lj_send,
    lj_recv,
    m_q,
    m_do,
    m_kv,
    dkv,
    g_send,
    g_recv,
    loc_sem,
    qd_s,
    qd_r,
    kv_s,
    kv_r,
    st_s,
    st_r,
    yf_s,
    yf_r,
    p_s,
    p_r,
    rc_s,
    rc_r,
    rj_s,
    rj_r,
    lc_s,
    lc_r,
    lj_s,
    lj_r,
    g_s,
    g_r,
):
    f32, bf16 = jnp.float32, jnp.bfloat16
    me = lax.axis_index("dp")
    mp = lax.axis_index("mp")
    group, y = mp // SHARE, mp % SHARE
    z, core = me // 2, me % 2
    nz = n // 2
    rows = n * BR
    per_class = n // SHARE

    column = pl.ds(pl.multiple_of(group * HD, HD), HD)
    loads = [
        (order_hbm, order_ref),
        (q_hbm, q_ref),
        (do_hbm, do_ref),
        (k_hbm.at[:, :, column], kv_in.at[0]),
        (v_hbm.at[:, :, column], kv_in.at[1]),
        (o_hbm, o_ref),
        (lse_hbm, lse_ref),
        (lg_hbm, lg_v),
        (fb_hbm, fb_v),
    ]
    loads = [pltpu.make_async_copy(a, b, loc_sem.at[i]) for i, (a, b) in enumerate(loads)]
    for load in loads:
        load.start()

    barrier = pltpu.get_barrier_semaphore()

    def greet_dp(k, _):
        pl.semaphore_signal(barrier, 1, device_id=((me + k) % n, mp), device_id_type=MESH)
        return 0

    def greet_mp(k, _):
        pl.semaphore_signal(barrier, 1, device_id=(me, (mp + k) % nm), device_id_type=MESH)
        return 0

    lax.fori_loop(1, n, greet_dp, 0)
    lax.fori_loop(1, nm, greet_mp, 0)

    for load in loads[:3]:
        load.wait()

    pl.semaphore_wait(barrier, n - 1 + nm - 1)

    def kv_slot(source, dest):
        return ((source + dest) % SHARE) * per_class + source // SHARE

    has_self = (me + me) % SHARE == y

    def send_kv(j, _):
        d = SHARE * ((me // SHARE + 7 * j) % per_class) + (y + SHARE - me % SHARE) % SHARE
        slot = y * per_class + me // SHARE
        block = order_ref[0, d]
        kv_send[d] = jnp.concatenate([kv_in[0, block], kv_in[1, block]], axis=0)

        @pl.when(d == me)
        def _():
            pltpu.make_async_copy(kv_send.at[me], kv_recv.at[slot], kv_r).start()

        @pl.when(d != me)
        def _():
            pltpu.make_async_remote_copy(
                kv_send.at[d], kv_recv.at[slot], kv_s, kv_r, device_id=(d, mp), device_id_type=MESH
            ).start()

        return 0


    def pack(d):
        block = order_ref[0, d]
        qb = q_ref[block]
        db = do_ref[block]
        qd_send[d] = jnp.concatenate([qb[:, :HD], qb[:, HD:], db[:, :HD], db[:, HD:]], axis=0)

    pack(me)
    pltpu.make_async_copy(qd_send.at[me], qd_recv.at[me], qd_r).start()

    def send_to(chip, other_core):
        d = (z + chip + nz) % nz * 2 + (core + other_core) % 2
        pack(d)
        pltpu.make_async_remote_copy(
            qd_send.at[d], qd_recv.at[me], qd_s, qd_r, device_id=(d, mp), device_id_type=MESH
        ).start()

    half = nz // 2
    most = 4 * (half - 2)

    def send_block(t, _):
        pair, sub = t // 8, t % 8
        near = sub // 2 % 2
        distance = (1 - near) * (half - 1 - pair) + near * (1 + pair)
        send_to((1 - 2 * (sub % 2)) * distance, sub // 4)
        return 0

    def send_middle(t, _):
        send_to((1 - 2 * (t % 2)) * (half // 2), t // 2)
        return 0

    send_to(half, 0)
    send_to(0, 1)
    send_to(half, 1)
    lax.fori_loop(0, 4, send_middle, 0)
    first = min(FIRST, most)
    lax.fori_loop(0, first, send_block, 0)
    for load in loads[3:5]:
        load.wait()
    lax.fori_loop(0, per_class, send_kv, 0)

    for load in loads[5:7]:
        load.wait()
    product = do_ref[...].astype(f32).reshape(rows, HPD * HD) * o_ref[...].astype(f32)
    delta0 = jnp.sum(product[:, :HD], axis=1, keepdims=True)
    delta1 = jnp.sum(product[:, HD:], axis=1, keepdims=True)
    lse = jnp.concatenate(
        [lse_ref[...].astype(f32), jnp.zeros((HD - HPD, rows), f32)], axis=0
    ).T
    lane = lax.broadcasted_iota(jnp.int32, (rows, HD), 1)
    st_cols[...] = jnp.where(lane == 2, delta0, jnp.where(lane == 3, delta1, lse))
    packed = st_cols[pl.ds(0, n, stride=BR), :]
    for r in range(1, BR):
        packed = packed + pltpu.roll(st_cols[pl.ds(r, n, stride=BR), :], 4 * r, 1)
    st_rows[...] = packed

    def send_stats(t, _):
        d = (me + t * STRIDE) % n
        st_send[d] = st_rows[pl.ds(order_ref[0, d], 1), :]
        pltpu.make_async_remote_copy(
            st_send.at[d], st_recv.at[me], st_s, st_r, device_id=(d, mp), device_id_type=MESH
        ).start()
        return 0

    st_send[me] = st_rows[pl.ds(order_ref[0, me], 1), :]
    pltpu.make_async_copy(st_send.at[me], st_recv.at[me], st_r).start()
    lax.fori_loop(1, n, send_stats, 0)

    for load in loads[7:]:
        load.wait()
    partner = me + 1 - 2 * core

    def partner_copy(g):
        return pltpu.make_async_remote_copy(
            p_send.at[pl.ds(2 * g, 2)],
            p_recv.at[pl.ds(2 * g, 2)],
            p_s.at[g],
            p_r.at[g],
            device_id=(partner, mp),
            device_id_type=MESH,
        )

    def make_term(g, _):
        start = pl.multiple_of(g * 256, 256)
        term = lax.dot_general(
            lg_v[:, pl.ds(start, 256)],
            o_ref[...],
            (((0,), (0,)), ((), ())),
            preferred_element_type=f32,
        )
        term = term + fb_v[pl.ds(start, 256), :].astype(f32)
        spans = term.reshape(256 // CR, CR, HPD * HD)
        top = jnp.max(jnp.max(jnp.abs(spans), axis=1, keepdims=True), axis=2, keepdims=True)
        scale = (top + 1e-06).astype(bf16).astype(f32)
        level = (spans / scale).astype(bf16).astype(f32)
        value = (level * scale).reshape(4, 64, HPD * HD)
        for chip in range(2):
            even, odd = value[2 * chip], value[2 * chip + 1]
            own[2 * g + chip] = jnp.where(core == 0, even, odd)
            p_send[2 * g + chip] = jnp.where(core == 0, odd, even).astype(bf16)
        partner_copy(g).start()
        return 0

    lax.fori_loop(0, nz // 2, make_term, 0)

    def partner_wait(g, _):
        partner_copy(g).wait()
        return 0

    lax.fori_loop(0, nz // 2, partner_wait, 0)

    sides = (
        (1, nz // 2, rc_send, rc_recv, rj_send, rj_recv, rc_s, rc_r, rj_s, rj_r),
        (-1, nz // 2 - 1, lc_send, lc_recv, lj_send, lj_recv, lc_s, lc_r, lj_s, lj_r),
    )

    def chip_at(distance):
        return (z + distance % nz) % nz

    def device_at(distance):
        return (chip_at(distance) * 2 + core, mp)

    def own_sum(distance):
        chip = chip_at(distance)
        return own[chip] + p_recv[chip].astype(f32)

    def walk_count(limit, j):
        return len([k for k in range(nz) if SPAN * k + j <= limit])

    def walk_copy(side, t, k):
        sign, _, send, recv, _, _, s_sem, r_sem, _, _ = side
        return pltpu.make_async_remote_copy(
            send.at[t, k],
            recv.at[t, k],
            s_sem.at[t, k],
            r_sem.at[t, k],
            device_id=device_at(sign),
            device_id_type=MESH,
        )

    def jump_copy(side, u):
        sign, limit, _, _, send, recv, _, _, s_sem, r_sem = side
        last = u == walk_count(limit, 1) - 1
        return pltpu.make_async_remote_copy(
            send.at[u],
            recv.at[u],
            s_sem.at[u],
            r_sem.at[u],
            device_id=device_at(sign if last else sign * SPAN),
            device_id_type=MESH,
        )

    def walk(side, t):
        sign, limit, send, recv = side[:4]
        j = SPAN - t
        came = walk_count(limit, j + 1) if t > 0 else 0
        for k in reversed(range(walk_count(limit, j))):
            total = own_sum(sign * (SPAN * k + j))
            if k < came:
                walk_copy(side, t - 1, k).wait_recv()
                total = total + recv[t - 1, k].astype(f32)
            send[t, k] = total.astype(bf16)
            walk_copy(side, t, k).start()

    def jump(side, u):
        sign, limit, _, walked, send, recv = side[:6]
        k = walk_count(limit, 1) - 1 - u
        if k < 0:
            return
        total = own_sum(sign * (SPAN * k + 1))
        if k < walk_count(limit, 2):
            walk_copy(side, SPAN - 2, k).wait_recv()
            total = total + walked[SPAN - 2, k].astype(f32)
        if u > 0:
            jump_copy(side, u - 1).wait_recv()
            total = total + recv[u - 1].astype(f32)
        send[u] = total.astype(bf16)
        jump_copy(side, u).start()

    jumps = walk_count(nz // 2, 1)
    stage_count = SPAN - 1 + jumps
    before = min(BEFORE, stage_count)

    def stage(i):
        for side in sides:
            if i < SPAN - 1:
                walk(side, i)
            else:
                jump(side, i - (SPAN - 1))

    for i in range(min(PASS, before)):
        stage(i)
        lax.fori_loop(min(first + i * PER, most), min(first + (i + 1) * PER, most), send_block, 0)

    whole_wait(kv_recv.at[pl.ds(0, per_class)], kv_r)
    share = pl.ds(y * per_class, per_class)
    forwards = [
        pltpu.make_async_remote_copy(
            kv_recv.at[share],
            kv_recv.at[share],
            yf_s.at[t - 1],
            yf_r.at[t - 1],
            device_id=(me, group * SHARE + (y + t) % SHARE),
            device_id_type=MESH,
        )
        for t in range(1, SHARE)
    ]
    for forward in forwards:
        forward.start()

    for i in range(min(PASS, before), before):
        stage(i)
        lax.fori_loop(min(first + i * PER, most), min(first + (i + 1) * PER, most), send_block, 0)
    lax.fori_loop(min(first + before * PER, most), most, send_block, 0)

    for forward in forwards:
        forward.wait()

    def unpack_kv(i, _):
        parts = []
        for b in range(2):
            source = order_ref[0, n + 2 * i + b]
            parts.append(kv_recv[kv_slot(source, me)])
        at = pl.ds(pl.multiple_of(2 * BR * i, 2 * BR), 2 * BR)
        for j in range(2):
            m_kv[j, at, :] = jnp.concatenate([part[BR * j : BR * (j + 1)] for part in parts], axis=0)
        return 0

    lax.fori_loop(0, n // 2, unpack_kv, 0)

    whole_wait(st_recv, st_r)
    whole_wait(qd_recv, qd_r)

    def unpack(i, _):
        parts = []
        for b in range(2):
            source = order_ref[0, n + 2 * i + b]
            st_rows[pl.ds(2 * i + b, 1), :] = st_recv[source]
            parts.append(qd_recv[source])
        at = pl.ds(pl.multiple_of(2 * BR * i, 2 * BR), 2 * BR)
        for h in range(HPD):
            m_q[h, at, :] = jnp.concatenate([part[BR * h : BR * (h + 1)] for part in parts], axis=0)
            low = BR * (HPD + h)
            m_do[h, at, :] = jnp.concatenate([part[low : low + BR] for part in parts], axis=0)
        return 0

    lax.fori_loop(0, n // 2, unpack, 0)

    arrived = st_rows[...]
    st_cols[pl.ds(0, n, stride=BR), :] = arrived
    for r in range(1, BR):
        st_cols[pl.ds(r, n, stride=BR), :] = pltpu.roll(arrived, HD - 4 * r, 1)
    stats = st_cols[...].T[0:8]

    def segments(positions):
        end = order_ref[0, 2 * n]
        found = (positions >= end).astype(jnp.int32)
        for j in range(1, order_ref.shape[1] - 2 * n):
            end = end + order_ref[0, 2 * n + j]
            found = found + (positions >= end).astype(jnp.int32)
        return found

    factor = HD ** (-0.5)
    nt = (((1,), (1,)), ((), ()))
    tn = (((0,), (0,)), ((), ()))
    dkv[...] = jnp.zeros_like(dkv)
    half_rows = rows // 2
    for part in range(2):
        low, high = part * half_rows, (part + 1) * half_rows
        k_pos = lax.broadcasted_iota(jnp.int32, (high, 1), 0)
        q_pos = lax.broadcasted_iota(jnp.int32, (1, half_rows), 1) + low
        allowed = (segments(k_pos) == segments(q_pos)) & (k_pos <= q_pos)
        k_head = m_kv[0, 0:high, :]
        v_head = m_kv[1, 0:high, :]
        for h in range(HPD):
            q_head = m_q[h, low:high, :]
            do_head = m_do[h, low:high, :]
            scores = lax.dot_general(k_head, q_head, nt, preferred_element_type=f32) * factor
            probs = jnp.where(allowed, jnp.exp(scores - stats[h : h + 1, low:high]), 0.0)
            dkv[0:high, HD:] += jnp.dot(probs.astype(bf16), do_head, preferred_element_type=f32)
            dprobs = lax.dot_general(v_head, do_head, nt, preferred_element_type=f32)
            delta = stats[HPD + h : HPD + h + 1, low:high]
            dscores = (probs * (dprobs - delta) * factor).astype(bf16)
            dkv[0:high, :HD] += jnp.dot(dscores, q_head, preferred_element_type=f32)
            q_grad = lax.dot_general(dscores, k_head, tn, preferred_element_type=f32)
            qg_out[low:high, HD * h : HD * (h + 1)] = q_grad.astype(bf16)

    qg_store = pltpu.make_async_copy(qg_out, qg_ref, loc_sem.at[0])
    qg_store.start()

    kept = rows // nm
    g_send[...] = dkv[...].astype(bf16).reshape(nm, kept, 2 * HD)
    pltpu.make_async_copy(g_send.at[mp], g_recv.at[mp], g_r).start()

    def send_grad(k, _):
        other = (mp + k) % nm
        pltpu.make_async_remote_copy(
            g_send.at[other], g_recv.at[mp], g_s, g_r, device_id=(me, other), device_id_type=MESH
        ).start()
        return 0

    lax.fori_loop(1, nm, send_grad, 0)

    for i in range(before, stage_count):
        stage(i)
    total = own_sum(0)
    for side in sides:
        count = walk_count(side[1], 1)
        if count:
            jump_copy(side, count - 1).wait_recv()
            total = total + side[5][count - 1].astype(f32)
    wg_out[...] = total
    wg_store = pltpu.make_async_copy(wg_out, wg_ref, loc_sem.at[1])
    wg_store.start()

    whole_wait(qd_send.at[pl.ds(0, n - 1)], qd_s)
    whole_wait(st_send.at[pl.ds(0, n - 1)], st_s)

    @pl.when(has_self)
    def _():
        whole_wait(kv_send.at[pl.ds(0, per_class - 1)], kv_s)

    @pl.when(jnp.logical_not(has_self))
    def _():
        whole_wait(kv_send.at[pl.ds(0, per_class)], kv_s)

    for side in sides:
        for t in range(SPAN - 1):
            for k in range(walk_count(side[1], SPAN - t)):
                walk_copy(side, t, k).wait_send()
        for u in range(walk_count(side[1], 1)):
            jump_copy(side, u).wait_send()

    whole_wait(g_recv, g_r)
    groups = nm // SHARE
    for x in range(groups):
        total = g_recv[SHARE * x].astype(f32)
        for j in range(1, SHARE):
            total = total + g_recv[SHARE * x + j].astype(f32)
        total = total.astype(bf16)
        kvg_out[:, HD * x : HD * (x + 1)] = total[:, :HD]
        kvg_out[:, HD * (groups + x) : HD * (groups + x + 1)] = total[:, HD:]
    kvg_store = pltpu.make_async_copy(kvg_out, kvg_ref, loc_sem.at[2])
    kvg_store.start()
    whole_wait(g_send.at[pl.ds(0, nm - 1)], g_s)
    qg_store.wait()
    wg_store.wait()
    kvg_store.wait()


def body(
    queries,
    keys,
    values,
    attn_out,
    out_grad,
    lse,
    layer_grad,
    feedback,
    doc_lengths,
    src_order,
    dst_order,
):
    n, nm = lax.axis_size("dp"), lax.axis_size("mp")
    rows, cols = queries.shape
    nz = n // 2
    jumps = -(-(nz // 2) // SPAN)
    kept = rows // nm
    owned = layer_grad.shape[1] // n
    f32, bf16 = jnp.float32, jnp.bfloat16
    hbm = pl.BlockSpec(memory_space=pltpu.HBM)
    dma = pltpu.SemaphoreType.DMA
    walks = [pltpu.VMEM((SPAN - 1, jumps, owned, cols), bf16)] * 2
    walks += [pltpu.VMEM((jumps, owned, cols), bf16)] * 2
    walk_sems = [dma((SPAN - 1, jumps))] * 2 + [dma((jumps,))] * 2

    def blocks(array):
        return array.reshape(n, BR, array.shape[1])

    order = jnp.concatenate([src_order, dst_order, doc_lengths], axis=1)
    outs = (
        jax.ShapeDtypeStruct((rows, cols), bf16),
        jax.ShapeDtypeStruct((kept, 2 * keys.shape[1]), bf16),
        jax.ShapeDtypeStruct((owned, cols), f32),
    )
    return pl.pallas_call(
        functools.partial(kernel, n, nm),
        out_shape=outs,
        in_specs=[hbm] * 9,
        out_specs=(hbm, hbm, hbm),
        scratch_shapes=[
            *(pltpu.VMEM(out.shape, out.dtype) for out in outs),
            pltpu.SMEM(order.shape, jnp.int32),
            pltpu.VMEM((n, BR, cols), bf16),
            pltpu.VMEM((n, BR, cols), bf16),
            pltpu.VMEM((rows, cols), bf16),
            pltpu.VMEM((HPD, rows), bf16),
            pltpu.VMEM((2, n, BR, HD), bf16),
            pltpu.VMEM(layer_grad.shape, bf16),
            pltpu.VMEM(feedback.shape[1:], bf16),
            pltpu.VMEM((rows, HD), f32),
            pltpu.VMEM((n, HD), f32),
            pltpu.VMEM((n, 4 * BR, HD), bf16),
            pltpu.VMEM((n, 4 * BR, HD), bf16),
            pltpu.VMEM((n, 2 * BR, HD), bf16),
            pltpu.VMEM((n, 2 * BR, HD), bf16),
            pltpu.VMEM((n, 1, HD), f32),
            pltpu.VMEM((n, 1, HD), f32),
            pltpu.VMEM((nz, owned, cols), f32),
            pltpu.VMEM((nz, owned, cols), bf16),
            pltpu.VMEM((nz, owned, cols), bf16),
            *walks,
            *walks,
            pltpu.VMEM((HPD, rows, HD), bf16),
            pltpu.VMEM((HPD, rows, HD), bf16),
            pltpu.VMEM((2, rows, HD), bf16),
            pltpu.VMEM((rows, 2 * HD), f32),
            pltpu.VMEM((nm, kept, 2 * HD), bf16),
            pltpu.VMEM((nm, kept, 2 * HD), bf16),
            dma((9,)),
            dma,
            dma,
            dma,
            dma,
            dma,
            dma,
            dma((SHARE - 1,)),
            dma((SHARE - 1,)),
            dma((nz // 2,)),
            dma((nz // 2,)),
            *walk_sems,
            *walk_sems,
            dma,
            dma,
        ],
        compiler_params=pltpu.CompilerParams(
            collective_id=0, has_side_effects=True, vmem_limit_bytes=54784 * 1024
        ),
    )(
        order,
        blocks(queries),
        blocks(out_grad),
        attn_out,
        lse.T,
        blocks(keys),
        blocks(values),
        layer_grad,
        feedback[0],
    )


def solution(mesh):
    return jax.shard_map(
        body,
        mesh=mesh,
        in_specs=(
            P("dp", "mp"),
            P("dp", None),
            P("dp", None),
            P("dp", "mp"),
            P("dp", "mp"),
            P("dp", "mp"),
            P("dp", None),
            P("dp", None, "mp"),
            P("dp", None),
            P("dp", None),
            P("dp", None),
        ),
        out_specs=(P("dp", "mp"), P(("dp", "mp"), None), P("dp", "mp")),
        check_vma=False,
    )
```
